512 devices in a mesh: patch: 64 (over x, z_lo, core), heads: 8 (over z_hi, y).
Axes of the slice: x: 4, y: 4, z: 16 (z_hi: 2, z_lo: 8; z = z_hi * 8 + z_lo), core: 2. Of those that a mesh axis runs over, the one named last changes fastest.
Arguments:
- queries: bfloat16 [3072, 3072], P('patch', 'heads'), may hold values from -64 to 64
- stale_pairs: bfloat16 [3072, 2, 3072], P(None, None, 'heads'), may hold values from -6 to 6
- diff_codes: bfloat16 [3072, 2, 3072], P('patch', None, 'heads'), may hold values from -6 to 6
- block_scales: bfloat16 [3072, 24], P('patch', 'heads'), may hold values from 0.09 to 1
- residual: bfloat16 [3072, 5120], P('patch', 'heads'), may hold values from -6 to 6
- branch_gate: float32 [5120], P('heads'), may hold values from 0.5 to 2
- out_weight: bfloat16 [3072, 5120], P('heads', 'patch'), may hold values from -0.109375 to 0.109375
Outputs:
- block_out: bfloat16 [3072, 5120], P('patch', 'heads')
The draws below stay inside these ranges and needn't reach their ends.
All inputs are finite; a program needn't handle non-finite values.
Results may differ from the reference program's by a relative error of at most 0.0095.
Values may be sent and summed in bfloat16 or wider, within the bound.
A program may use at most 128 MiB of HBM per device.

```python
import math
import jax
import jax.numpy as jnp
from jax import lax

D = 5120
HD = 128
HEADS = 24
TOKENS = 3072


def mixed_law(sub_key, shape):
    normal_part = jax.random.truncated_normal(sub_key, -6.0, 6.0, shape, jnp.float32)
    return normal_part


def shared_draw(key):
    key_stale, key_codes, key_scales, key_query, key_rows, key_pick = jax.random.split(key, 6)
    width_all = HEADS * HD
    stale_all = mixed_law(key_stale, (TOKENS, 2, width_all))
    codes_all = mixed_law(key_codes, (TOKENS, 2, width_all))
    scales_all = jnp.exp(jax.random.uniform(key_scales, (TOKENS, HEADS), jnp.float32, math.log(0.1), 0.0))
    query_all = 2.2 * mixed_law(key_query, (TOKENS, width_all))
    query_rows = jax.random.randint(key_rows, (6,), 0, TOKENS)
    first_rows = jax.random.randint(key_pick, (6,), 0, TOKENS - 1)
    second_rows = first_rows + 1
    stale_all = stale_all.at[second_rows, 0].set(stale_all[second_rows, 0])
    codes_all = codes_all.at[second_rows, 0].set(codes_all[second_rows, 0])
    scales_all = scales_all.at[second_rows].set(scales_all[second_rows])
    query_all = query_all.at[query_rows].set(query_all[query_rows])
    return (stale_all, codes_all, scales_all, query_all)


def draw_queries(key, part):
    drawn = shared_draw(key)
    return drawn[3].astype(jnp.bfloat16)


def draw_stale_pairs(key, part):
    drawn = shared_draw(key)
    return drawn[0].astype(jnp.bfloat16)


def draw_diff_codes(key, part):
    drawn = shared_draw(key)
    return drawn[1].astype(jnp.bfloat16)


def draw_block_scales(key, part):
    drawn = shared_draw(key)
    return drawn[2].astype(jnp.bfloat16)


def block_scale(stream_key, dims, cuts, smallest, top_value):
    def one(axis_at, shards_of):
        steps = jax.random.uniform(jax.random.fold_in(jax.random.fold_in(stream_key, 6), axis_at), (shards_of,), jnp.float32, smallest / len(cuts), top_value / len(cuts))
        return jnp.repeat(jnp.exp(steps), dims[axis_at] // shards_of).reshape((-1,) + (1,) * (len(dims) - axis_at - 1))

    loudness = one(*cuts[0])
    for cut in cuts[1:]:
        loudness = loudness * one(*cut)
    return loudness


def normal_values(own_key, shape, spread, bound, cuts=(), held_as=jnp.bfloat16):
    values = jax.random.normal(own_key, shape, jnp.float32) * spread
    if len(cuts) > 0:
        values = block_scale(own_key, shape, cuts, -0.22, 0.18) * values
    return jnp.clip(values, min=-bound, max=bound).astype(held_as)


def setup_inputs(seed: int = 0) -> dict:
    key_of = jax.random.split(jax.random.key(seed), 8)
    return {
        "queries": draw_queries(jax.random.fold_in(key_of[7], 71), 0),
        "stale_pairs": draw_stale_pairs(jax.random.fold_in(key_of[7], 71), 0),
        "diff_codes": draw_diff_codes(jax.random.fold_in(key_of[7], 71), 0),
        "block_scales": draw_block_scales(jax.random.fold_in(key_of[7], 71), 0),
        "residual": normal_values(key_of[4], (TOKENS, D), 1.0, 6.0, ((0, 64), (1, 8))),
        "branch_gate": jnp.clip(0.5 + 1.5 * jax.random.uniform(key_of[5], (D,), jnp.float32) ** block_scale(key_of[5], (D,), ((0, 8),), -0.2, 0.2), 0.5, 2.0),
        "out_weight": normal_values(key_of[6], (HEADS * HD, D), (HEADS * HD) ** -0.5, 0.109375, ((0, 8), (1, 64))),
    }


def one_head(operands):
    query_rows, key_rows, value_rows = operands
    scores = jnp.dot(query_rows, key_rows.T, preferred_element_type=jnp.float32) * (1.0 / math.sqrt(HD))
    row_max = lax.optimization_barrier(jnp.max(scores, axis=1, keepdims=True))
    exponent = jnp.exp(scores - row_max)
    probs = exponent.astype(jnp.bfloat16)
    summed = jnp.dot(probs, value_rows, preferred_element_type=jnp.float32)
    return (summed / lax.optimization_barrier(jnp.sum(exponent, axis=1, keepdims=True))).astype(jnp.bfloat16)

def reference(queries, stale_pairs, diff_codes, block_scales, residual, branch_gate, out_weight):
    scale_full = jnp.repeat(block_scales.astype(jnp.float32), HD, axis=1)
    rebuilt = (stale_pairs.astype(jnp.float32) + scale_full[:, None, :] * diff_codes.astype(jnp.float32)).astype(jnp.bfloat16)
    key_heads = rebuilt[:, 0].reshape(TOKENS, HEADS, HD).transpose(1, 0, 2)
    value_heads = rebuilt[:, 1].reshape(TOKENS, HEADS, HD).transpose(1, 0, 2)
    query_heads = queries.reshape(TOKENS, HEADS, HD).transpose(1, 0, 2)
    attended = lax.map(one_head, (query_heads, key_heads, value_heads))
    attended = attended.transpose(1, 0, 2).reshape(TOKENS, HEADS * HD)
    projected = jnp.dot(attended, out_weight, preferred_element_type=jnp.float32)
    return (residual.astype(jnp.float32) + branch_gate[None, :] * projected).astype(jnp.bfloat16)
```

```python
import functools
import math

import jax
import jax.numpy as jnp
from jax import lax
from jax.experimental import pallas as pl
from jax.experimental.pallas import tpu as pltpu
from jax.sharding import PartitionSpec as P

MESH = pl.DeviceIdType.MESH
BF16, F32 = jnp.bfloat16, jnp.float32
ROWS, FEAT, HD, NH = 48, 384, 128, 3
COLS, SHARD = 640, 80
KEYS = 1536
NT = (((1,), (1,)), ((), ()))


def place(x, y, z, zh, c):
    return ((x * 8 + z) * 2 + c, zh * 4 + y)


def kernel(
    q_ref, kv_ref, wt_ref, res_ref, gate_ref, out_ref,
    kv, qb, osend, orecv, att, arecv, part, psend, precv, wb,
    k_send, k_recv, kd_send, kd_recv, w_send, w_recv, wd_sem, q_sem, o_send, o_recv,
    a_send, a_recv, p_send, p_recv,
):
    p, h = lax.axis_index("patch"), lax.axis_index("heads")
    c = lax.rem(p, 2)
    z = lax.rem(lax.div(p, 2), 8)
    x = lax.div(p, 16)
    y = lax.rem(h, 4)
    zh = lax.div(h, 4)
    z0 = lax.rem(z, 4)
    z1 = lax.div(z, 4)
    half = z1 * 4

    x_mates = [lax.rem(x + d, 4) for d in (1, 3, 2)]
    z_mates = [z0 + 1 - 2 * lax.rem(z0, 2), lax.rem(z0 + 2, 4), 3 - z0]
    core_dev = place(x, y, z, zh, 1 - c)
    x_devs = [place(m, y, z, zh, c) for m in x_mates]
    z_devs = [place(x, y, half + m, zh, c) for m in z_mates]
    across = lax.rem(z + 4, 8)
    g4 = place(x, y, across, zh, c)
    g8 = place(x, y, z, 1 - zh, c)
    g12 = place(x, y, across, 1 - zh, c)

    to_z = zh * 4 + z0
    w_to = place(y, lax.rem(x, 2) * 2 + z1, to_z, lax.div(x, 2), c)
    w_from = place(zh * 2 + lax.div(y, 2), x, lax.rem(y, 2) * 4 + z0, z1, c)
    w_self = (w_to[0] == p) & (w_to[1] == h)

    a_planes = [lax.rem(y + d, 4) for d in range(4)]
    a_to = [place(y, m, z, zh, c) for m in a_planes]
    a_from = [place(m, x, z, zh, c) for m in (x, *x_mates)]
    diag = x == y

    barrier = pltpu.get_barrier_semaphore()

    def greet(target):
        pl.semaphore_signal(barrier, inc=1, device_id=target, device_id_type=MESH)

    for target in [core_dev, *x_devs, *z_devs, g4, g8, g12, *a_to[1:], *a_from[1:]]:
        greet(target)

    @pl.when(jnp.logical_not(diag))
    def _():
        greet(a_to[0])
        greet(a_from[0])

    @pl.when(jnp.logical_not(w_self))
    def _():
        greet(w_to)
        greet(w_from)

    kv[c, x, z0] = kv_ref[...]
    qb[0] = q_ref[...]
    pl.semaphore_wait(
        barrier, 16 + 2 * (1 - diag.astype(jnp.int32)) + 2 * (1 - w_self.astype(jnp.int32))
    )

    def remote(src, dst, send, recv, target):
        return pltpu.make_async_remote_copy(
            src_ref=src, dst_ref=dst, send_sem=send, recv_sem=recv,
            device_id=target, device_id_type=MESH,
        )

    sent = []

    def start(copy):
        copy.start()
        sent.append(copy)

    for i, target in enumerate(z_devs):
        block = kv.at[c, x, z0]
        start(remote(block, block, k_send.at[i], k_recv.at[x, z0], target))
    q_copy = remote(qb.at[0], qb.at[1], q_sem.at[0], q_sem.at[1], g4)
    start(q_copy)

    def along_x(zs, k):
        block = kv.at[c, x, zs]
        for i, target in enumerate(x_devs):
            start(remote(block, block, k_send.at[3 + 3 * k + i], k_recv.at[x, zs], target))

    def to_core(xs, zs, k):
        block = kv.at[c, xs, zs]
        start(remote(block, block, kd_send.at[k], kd_recv.at[xs, zs], core_dev))

    along_x(z0, 0)
    to_core(x, z0, 0)

    mine = wb.at[c, z]
    w_copy = remote(wt_ref, wb.at[c, to_z], w_send.at[0], w_recv.at[8], w_to)
    w_local = pltpu.make_async_copy(wt_ref, wb.at[c, to_z], w_recv.at[8])

    @pl.when(w_self)
    def _():
        w_local.start()

    @pl.when(jnp.logical_not(w_self))
    def _():
        w_copy.start()

    def arrived(block, sem):
        pltpu.make_async_copy(block, block, sem).wait()

    for k, zs in enumerate(z_mates):
        arrived(kv.at[c, x, zs], k_recv.at[x, zs])
        along_x(zs, k + 1)
        to_core(x, zs, k + 1)

    arrived(mine, w_recv.at[8])
    for i, target in enumerate(z_devs):
        start(remote(mine, mine, w_send.at[1 + i], w_recv.at[z], target))
    start(remote(mine, mine, w_send.at[4], w_recv.at[z], g4))

    k = 4
    for zs in (z0, *z_mates):
        for xs in x_mates:
            arrived(kv.at[c, xs, zs], k_recv.at[xs, zs])
            to_core(xs, zs, k)
            k += 1

    q_copy.wait_recv()
    for zs in (z0, *z_mates):
        for xs in (x, *x_mates):
            arrived(kv.at[1 - c, xs, zs], kd_recv.at[xs, zs])

    lane = lax.broadcasted_iota(jnp.int32, (2 * ROWS, HD), 1)
    stats = jnp.zeros((2 * ROWS, HD), F32)
    for e in range(NH):
        query = qb[:, :, e * HD : (e + 1) * HD].reshape(2 * ROWS, HD)
        keys = kv[:, :, :, :, e * HD : (e + 1) * HD].reshape(KEYS, HD)
        values = kv[:, :, :, :, FEAT + e * HD : FEAT + (e + 1) * HD].reshape(KEYS, HD)
        scores = lax.dot_general(query, keys, NT, preferred_element_type=F32)
        scores = scores * (1.0 / math.sqrt(HD))
        top = jnp.max(scores, axis=1, keepdims=True)
        exponent = jnp.exp(scores - top)
        total = jnp.sum(exponent, axis=1, keepdims=True)
        mixed = jnp.dot(exponent.astype(BF16), values, preferred_element_type=F32) / total
        osend[:, :, e * HD : (e + 1) * HD] = mixed.astype(BF16).reshape(2, ROWS, HD)
        level = top + jnp.log(total)
        for t in range(3):
            term = level.astype(BF16).astype(F32)
            stats = jnp.where(lane == 3 * e + t, term, stats)
            level = level - term
    osend[:, :, FEAT:] = stats.astype(BF16).reshape(2, ROWS, HD)

    o_copies = [
        remote(osend.at[1], orecv.at[0], o_send.at[0], o_recv.at[0], g4),
        remote(osend.at[0], orecv.at[1], o_send.at[1], o_recv.at[1], g8),
        remote(osend.at[1], orecv.at[2], o_send.at[2], o_recv.at[2], g12),
    ]
    for copy in (o_copies[1], o_copies[2], o_copies[0]):
        start(copy)

    arrived(wb.at[c, across], w_recv.at[across])
    for i, target in enumerate(z_devs):
        block = wb.at[c, across]
        start(remote(block, block, w_send.at[5 + i], w_recv.at[across], target))

    def merge(one, two):
        pieces = []
        for e in range(NH):
            levels = []
            for part_of in (one, two):
                terms = [part_of[:, FEAT + 3 * e + t : FEAT + 3 * e + t + 1].astype(F32) for t in range(3)]
                levels.append(terms[0] + terms[1] + terms[2])
            high = jnp.maximum(levels[0], levels[1])
            w1, w2 = jnp.exp(levels[0] - high), jnp.exp(levels[1] - high)
            at = slice(e * HD, (e + 1) * HD)
            blend = one[:, at].astype(F32) * w1 + two[:, at].astype(F32) * w2
            pieces.append((blend / (w1 + w2)).astype(BF16))
        return jnp.concatenate(pieces, axis=1)

    o_copies[0].wait_recv()
    att[zh] = merge(osend[0], orecv[0])
    o_copies[1].wait_recv()
    o_copies[2].wait_recv()
    att[1 - zh] = merge(orecv[1], orecv[2])

    a_local = pltpu.make_async_copy(att, arecv.at[x], a_recv.at[x])
    a_copies = [remote(att, arecv.at[x], a_send.at[d], a_recv.at[x], a_to[d]) for d in range(4)]
    for copy in a_copies[1:]:
        start(copy)

    @pl.when(diag)
    def _():
        a_local.start()

    @pl.when(jnp.logical_not(diag))
    def _():
        a_copies[0].start()

    for d in range(1, 4):
        for base in (half, 4 - half):
            zs = base + z_mates[d - 1]
            arrived(wb.at[c, zs], w_recv.at[zs])
    w_core = remote(wb.at[c], wb.at[c], wd_sem.at[0], wd_sem.at[1], core_dev)
    start(w_core)
    arrived(wb.at[1 - c], wd_sem.at[1])

    for m in (x, *x_mates):
        arrived(arecv.at[m], a_recv.at[m])
    total = None
    for side in range(2):
        weight = jnp.concatenate([wb[j % 2, side * 4 + j // 2] for j in range(8)], axis=0)
        rows = arecv[:, side].reshape(4 * ROWS, FEAT)
        term = lax.dot_general(rows, weight, NT, preferred_element_type=F32)
        total = term if total is None else total + term
    part[...] = total.reshape(4, ROWS, COLS)
    psend[...] = total.astype(BF16).reshape(4, ROWS, COLS)
    for i, (m, target) in enumerate(zip(x_mates, x_devs)):
        start(remote(psend.at[m], precv.at[x], p_send.at[i], p_recv.at[x], target))
    summed = part[x]
    for m in x_mates:
        arrived(precv.at[m], p_recv.at[m])
        summed = summed + precv[m].astype(F32)
    out_ref[...] = (res_ref[...].astype(F32) + gate_ref[...] * summed).astype(BF16)

    for copy in sent:
        copy.wait_send()

    @pl.when(jnp.logical_not(w_self))
    def _():
        w_copy.wait_send()

    @pl.when(jnp.logical_not(diag))
    def _():
        a_copies[0].wait_send()


def body(queries, stale_pairs, diff_codes, block_scales, residual, branch_gate, out_weight):
    first = lax.axis_index("patch") * ROWS
    stale = lax.dynamic_slice_in_dim(stale_pairs, first, ROWS, axis=0)
    scale = jnp.repeat(block_scales.astype(F32), HD, axis=1)[:, None, :]
    rebuilt = (stale.astype(F32) + scale * diff_codes.astype(F32)).astype(BF16)
    rebuilt = jnp.concatenate([rebuilt[:, 0], rebuilt[:, 1]], axis=1)
    dma = pltpu.SemaphoreType.DMA
    return pl.pallas_call(
        kernel,
        out_shape=jax.ShapeDtypeStruct((ROWS, COLS), BF16),
        in_specs=[pl.BlockSpec(memory_space=pltpu.VMEM)] * 5,
        out_specs=pl.BlockSpec(memory_space=pltpu.VMEM),
        scratch_shapes=[
            pltpu.VMEM((2, 4, 4, ROWS, 2 * FEAT), BF16),
            pltpu.VMEM((2, ROWS, FEAT), BF16),
            pltpu.VMEM((2, ROWS, FEAT + HD), BF16),
            pltpu.VMEM((3, ROWS, FEAT + HD), BF16),
            pltpu.VMEM((2, ROWS, FEAT), BF16),
            pltpu.VMEM((4, 2, ROWS, FEAT), BF16),
            pltpu.VMEM((4, ROWS, COLS), F32),
            pltpu.VMEM((4, ROWS, COLS), BF16),
            pltpu.VMEM((4, ROWS, COLS), BF16),
            pltpu.VMEM((2, 8, SHARD, FEAT), BF16),
            dma((15,)), dma((4, 4)), dma((16,)), dma((4, 4)), dma((8,)), dma((9,)), dma((2,)),
            dma((2,)), dma((3,)), dma((3,)), dma((4,)), dma((4,)), dma((3,)), dma((4,)),
        ],
        compiler_params=pltpu.CompilerParams(
            collective_id=0, has_side_effects=True, vmem_limit_bytes=40 << 20
        ),
        name="block_attention",
    )(queries, rebuilt, out_weight.T, residual, branch_gate.reshape(1, COLS))


def solution(mesh):
    in_specs = (
        P("patch", "heads"),
        P(None, None, "heads"),
        P("patch", None, "heads"),
        P("patch", "heads"),
        P("patch", "heads"),
        P("heads"),
        P("heads", "patch"),
    )
    return jax.shard_map(
        body, mesh=mesh, in_specs=in_specs, out_specs=P("patch", "heads"), check_vma=False
    )
```

```python
import functools
import math

import jax
import jax.numpy as jnp
from jax import lax
from jax.experimental import pallas as pl
from jax.experimental.pallas import tpu as pltpu
from jax.sharding import PartitionSpec as P

MESH = pl.DeviceIdType.MESH
BF16, F32 = jnp.bfloat16, jnp.float32
ROWS, FEAT, HD, NH = 48, 384, 128, 3
COLS, SHARD = 640, 80
KEYS = 1536
NT = (((1,), (1,)), ((), ()))


def place(x, y, z, zh, c):
    return ((x * 8 + z) * 2 + c, zh * 4 + y)


def kernel(
    q_ref, kv_ref, wt_ref, res_ref, gate_ref, out_ref,
    kvs, kv, qb, osend, orecv, arecv, wcol, wt_far, we, acc, psend, precv,
    k_send, k_recv, kd_send, kd_recv, q_send, q_recv, w_send, w_recv, x_send, x_recv, wd_send, wd_recv,
    o_send, o_recv, a_send, a_recv, p_send, p_recv, far_sem,
):
    p, h = lax.axis_index("patch"), lax.axis_index("heads")
    c = lax.rem(p, 2)
    z = lax.rem(lax.div(p, 2), 8)
    x = lax.div(p, 16)
    y = lax.rem(h, 4)
    zh = lax.div(h, 4)
    z0 = lax.rem(z, 4)
    z1 = lax.div(z, 4)
    half = z1 * 4
    other = 4 - half
    across = lax.rem(z + 4, 8)
    worker = x < NH

    x_mates = [lax.rem(x + d, 4) for d in (1, 3, 2)]
    y_mates = [lax.rem(y + d, 4) for d in (1, 3, 2)]
    z_mates = [z0 + 1 - 2 * lax.rem(z0, 2), 3 - z0, lax.rem(z0 + 2, 4)]
    core_dev = place(x, y, z, zh, 1 - c)
    y_devs = [place(x, m, z, zh, c) for m in y_mates]
    z_devs = [place(x, y, half + m, zh, c) for m in z_mates]
    g4 = place(x, y, across, zh, c)
    g8 = place(x, y, z, 1 - zh, c)
    g12 = place(x, y, across, 1 - zh, c)

    sender = lax.div(x, 2) == zh
    w_to = [place(y, lax.rem(x, 2) * 2 + side, z, zh, c) for side in (z1, 1 - z1)]
    w_from = place(zh * 2 + lax.div(y, 2), x, z, zh, c)
    w_self = [sender & (x == y) & (y == lax.rem(x, 2) * 2 + side) for side in (z1, 1 - z1)]
    w_own = w_self[0] | w_self[1]

    barrier = pltpu.get_barrier_semaphore()

    def greet(target):
        pl.semaphore_signal(barrier, inc=1, device_id=target, device_id_type=MESH)

    for target in [g12, g4, *[place(m, y, across, zh, c) for m in x_mates], *y_devs, core_dev]:
        greet(target)
    for m in (x, *x_mates):
        for target in z_mates:
            greet(place(m, y, half + target, zh, c))
    for m in x_mates:
        greet(place(m, y, z, zh, c))

    @pl.when(jnp.logical_not(w_own))
    def _():
        greet(w_from)

    for i in range(2):
        @pl.when(sender & jnp.logical_not(w_self[i]))
        def _():
            greet(w_to[i])

    for e in range(NH):
        kvs[e, :, :HD] = kv_ref[:, e * HD : (e + 1) * HD]
        kvs[e, :, HD:] = kv_ref[:, FEAT + e * HD : FEAT + (e + 1) * HD]
    own_count = w_own.astype(jnp.int32)
    pl.semaphore_wait(barrier, 25 - 2 * own_count + 2 * sender.astype(jnp.int32))
    pl.semaphore_signal(far_sem, inc=1, device_id=g4, device_id_type=MESH)

    def remote(src, dst, send, recv, target):
        return pltpu.make_async_remote_copy(
            src_ref=src, dst_ref=dst, send_sem=send, recv_sem=recv,
            device_id=target, device_id_type=MESH,
        )

    sent, sent_if = [], []

    def start(copy):
        copy.start()
        sent.append(copy)

    def start_if(condition, copy):
        @pl.when(condition)
        def _():
            copy.start()

        sent_if.append((condition, copy))

    def arrived(block, sem):
        pltpu.make_async_copy(block, block, sem).wait()

    def head_of(e):
        return slice(e * HD, (e + 1) * HD)

    start_if(jnp.logical_not(sender), remote(wt_ref, wt_far, w_send.at[0], w_recv.at[8], g12))
    mine = wcol.at[z]
    w_src = [wt_ref, wt_far]

    def send_shard(i):
        start_if(
            sender & jnp.logical_not(w_self[i]),
            remote(w_src[i], mine, w_send.at[1 + i], w_recv.at[9], w_to[i]),
        )

        @pl.when(w_self[i])
        def _():
            pltpu.make_async_copy(w_src[i], mine, w_recv.at[9]).start()

    send_shard(0)

    for k, m in enumerate((*z_mates[::-1], z0)):
        for e in range(NH):
            copy = remote(
                kvs.at[e], kv.at[c, z0, x], k_send.at[k, e], k_recv.at[z0, x], place(e, y, half + m, zh, c)
            )
            if k < 3:
                start(copy)
            else:
                start_if(x != e, copy)

                @pl.when(x == e)
                def _():
                    pltpu.make_async_copy(kvs.at[e], kv.at[c, z0, x], k_recv.at[z0, x]).start()

    for row, to_z in enumerate((across, z)):
        row = 1 - row
        for e in range(NH):
            copy = remote(
                q_ref.at[:, head_of(e)], qb.at[row, x], q_send.at[row, e], q_recv.at[row, x],
                place(e, y, to_z, zh, c),
            )
            if row == 1:
                start(copy)
            else:
                start_if(x != e, copy)

                @pl.when(x == e)
                def _():
                    pltpu.make_async_copy(q_ref.at[:, head_of(e)], qb.at[0, x], q_recv.at[0, x]).start()

    @pl.when(sender)
    def _():
        arrived(wt_far, w_recv.at[8])

    send_shard(1)

    order = (z0, *z_mates)
    for k, zs in enumerate(order):
        @pl.when(worker)
        def _():
            for m in (x, *x_mates):
                arrived(kv.at[c, zs, m], k_recv.at[zs, m])

        block = kv.at[c, zs]
        start_if(worker, remote(block, block, kd_send.at[k], kd_recv.at[zs], core_dev))
        if k == 1:
            arrived(mine, w_recv.at[9])
            for i, target in enumerate(z_devs):
                start(remote(mine, mine, w_send.at[3 + i], w_recv.at[z], target))
            start(remote(mine, mine, w_send.at[6], w_recv.at[z], g4))

    @pl.when(worker)
    def _():
        for row in range(2):
            for m in (x, *x_mates):
                arrived(qb.at[row, m], q_recv.at[row, m])
        for zs in order:
            arrived(kv.at[1 - c, zs], kd_recv.at[zs])
        keys = kv[:, :, :, :, :HD].reshape(KEYS, HD)
        values = kv[:, :, :, :, HD:].reshape(KEYS, HD)
        wide = lax.broadcasted_iota(jnp.int32, (4 * ROWS, 2 * HD), 1)
        deep = lax.broadcasted_iota(jnp.int32, (4 * ROWS, 2 * HD), 0)
        at_row = lax.broadcasted_iota(jnp.int32, (16, HD), 0)
        for row in range(2):
            levels = []
            for pair in range(2):
                query = qb[row, 2 * pair : 2 * pair + 2].reshape(2 * ROWS, HD)
                scores = lax.dot_general(query, keys, NT, preferred_element_type=F32)
                scores = scores * (1.0 / math.sqrt(HD))
                top = jnp.max(scores, axis=1, keepdims=True)
                exponent = jnp.exp(scores - top)
                total = jnp.sum(exponent, axis=1, keepdims=True)
                mixed = jnp.dot(exponent.astype(BF16), values, preferred_element_type=F32) / total
                osend[row, 2 * pair * ROWS : 2 * (pair + 1) * ROWS] = mixed.astype(BF16)
                levels.append(top + jnp.log(total))
            level = jnp.concatenate(levels, axis=0)
            stats = jnp.zeros((16, HD), F32)
            for t in range(3):
                term = level.astype(BF16).astype(F32)
                level = level - term
                line = jnp.sum(jnp.where(wide == deep, term, 0.0), axis=0, keepdims=True)
                stats = jnp.where(at_row == 2 * t, line[:, :HD], stats)
                stats = jnp.where(at_row == 2 * t + 1, line[:, HD:], stats)
            osend[row, 4 * ROWS :] = stats.astype(BF16)

    pl.semaphore_wait(far_sem, 1)
    for i, (row, target) in enumerate(((0, g8), (1, g12), (1, g4))):
        start_if(worker, remote(osend.at[row], orecv.at[i], o_send.at[i], o_recv.at[i], target))

    def scatter(base, g):
        for e in range(NH):
            block = wcol.at[pl.ds(base, 4), :, head_of(e)]
            dst = we.at[c, x, pl.ds(base, 4)]
            start_if(x != e, remote(block, dst, x_send.at[g, e], x_recv.at[g, x], place(e, y, z, zh, c)))

            @pl.when(x == e)
            def _():
                pltpu.make_async_copy(block, dst, x_recv.at[g, x]).start()

    for m in z_mates:
        arrived(wcol.at[half + m], w_recv.at[half + m])
    scatter(half, 0)
    arrived(wcol.at[across], w_recv.at[across])
    for i, target in enumerate(z_devs):
        block = wcol.at[across]
        start(remote(block, block, w_send.at[7 + i], w_recv.at[across], target))

    def to_core(base, g):
        @pl.when(worker)
        def _():
            for m in (x, *x_mates):
                arrived(we.at[c, m, pl.ds(base, 4)], x_recv.at[g, m])

        block = we.at[c, :, pl.ds(base, 4)]
        start_if(worker, remote(block, block, wd_send.at[g], wd_recv.at[g], core_dev))

    to_core(half, 0)
    for m in z_mates:
        arrived(wcol.at[other + m], w_recv.at[other + m])
    scatter(other, 1)

    def merge(one, two):
        wide = lax.broadcasted_iota(jnp.int32, (4 * ROWS, 2 * HD), 1)
        deep = lax.broadcasted_iota(jnp.int32, (4 * ROWS, 2 * HD), 0)
        levels = []
        for part_of in (one, two):
            stats = part_of[4 * ROWS :].astype(F32)
            line = jnp.concatenate([stats[i : i + 1] + stats[i + 2 : i + 3] + stats[i + 4 : i + 5] for i in range(2)], axis=1)
            levels.append(jnp.sum(jnp.where(wide == deep, line, 0.0), axis=1, keepdims=True))
        high = jnp.maximum(levels[0], levels[1])
        w1, w2 = jnp.exp(levels[0] - high), jnp.exp(levels[1] - high)
        blend = one[: 4 * ROWS].astype(F32) * w1 + two[: 4 * ROWS].astype(F32) * w2
        return (blend / (w1 + w2)).astype(BF16)

    @pl.when(worker)
    def _():
        arrived(orecv.at[2], o_recv.at[2])
        arecv[y, zh] = merge(osend[0], orecv[2])
        arrived(orecv.at[0], o_recv.at[0])
        arrived(orecv.at[1], o_recv.at[1])
        arecv[y, 1 - zh] = merge(orecv[0], orecv[1])

    for i, target in enumerate(y_devs):
        block = arecv.at[y]
        start_if(worker, remote(block, block, a_send.at[i], a_recv.at[y], target))

    to_core(other, 1)

    @pl.when(worker)
    def _():
        arrived(we.at[1 - c, :, pl.ds(half, 4)], wd_recv.at[0])
        arrived(we.at[1 - c, :, pl.ds(other, 4)], wd_recv.at[1])
        for m in y_mates:
            arrived(arecv.at[m], a_recv.at[m])
        rows, weights = [], []
        for m in range(4):
            for side in range(2):
                same = 1 - lax.rem(y + side, 2)
                rows.append(arecv[m, same * zh + (1 - same) * (1 - zh)])
                weights.append(jnp.concatenate([we[j % 2, m, side * 4 + j // 2] for j in range(8)], axis=0))
        total = lax.dot_general(
            jnp.concatenate(rows, axis=1), jnp.concatenate(weights, axis=1), NT, preferred_element_type=F32
        )
        psend[...] = total.astype(BF16).reshape(4, ROWS, COLS)
        for e in range(NH):
            @pl.when(x == e)
            def _():
                acc[...] = total[e * ROWS : (e + 1) * ROWS]

    @pl.when(jnp.logical_not(worker))
    def _():
        acc[...] = jnp.zeros((ROWS, COLS), F32)

    for i, m in enumerate(x_mates):
        start_if(worker, remote(psend.at[m], precv.at[x], p_send.at[i], p_recv.at[x], place(m, y, z, zh, c)))
    for e in range(NH):
        @pl.when(x != e)
        def _():
            arrived(precv.at[e], p_recv.at[e])
            acc[...] += precv[e].astype(F32)

    out_ref[...] = (res_ref[...].astype(F32) + gate_ref[...] * acc[...]).astype(BF16)

    for copy in sent:
        copy.wait_send()
    for condition, copy in sent_if:
        @pl.when(condition)
        def _():
            copy.wait_send()


def body(queries, stale_pairs, diff_codes, block_scales, residual, branch_gate, out_weight):
    first = lax.axis_index("patch") * ROWS
    stale = lax.dynamic_slice_in_dim(stale_pairs, first, ROWS, axis=0)
    scale = jnp.repeat(block_scales.astype(F32), HD, axis=1)[:, None, :]
    rebuilt = (stale.astype(F32) + scale * diff_codes.astype(F32)).astype(BF16)
    rebuilt = jnp.concatenate([rebuilt[:, 0], rebuilt[:, 1]], axis=1)
    dma = pltpu.SemaphoreType.DMA
    return pl.pallas_call(
        kernel,
        out_shape=jax.ShapeDtypeStruct((ROWS, COLS), BF16),
        in_specs=[pl.BlockSpec(memory_space=pltpu.VMEM)] * 5,
        out_specs=pl.BlockSpec(memory_space=pltpu.VMEM),
        scratch_shapes=[
            pltpu.VMEM((NH, ROWS, 2 * HD), BF16),
            pltpu.VMEM((2, 4, 4, ROWS, 2 * HD), BF16),
            pltpu.VMEM((2, 4, ROWS, HD), BF16),
            pltpu.VMEM((2, 4 * ROWS + 16, HD), BF16),
            pltpu.VMEM((3, 4 * ROWS + 16, HD), BF16),
            pltpu.VMEM((4, 2, 4 * ROWS, HD), BF16),
            pltpu.VMEM((8, SHARD, FEAT), BF16),
            pltpu.VMEM((SHARD, FEAT), BF16),
            pltpu.VMEM((2, 4, 8, SHARD, HD), BF16),
            pltpu.VMEM((ROWS, COLS), F32),
            pltpu.VMEM((4, ROWS, COLS), BF16),
            pltpu.VMEM((NH, ROWS, COLS), BF16),
            dma((4, NH)), dma((4, 4)), dma((4,)), dma((4,)), dma((2, NH)), dma((2, 4)), dma((10,)), dma((10,)),
            dma((2, NH)), dma((2, 4)), dma((2,)), dma((2,)),
            dma((3,)), dma((3,)), dma((3,)), dma((4,)), dma((3,)), dma((3,)), pltpu.SemaphoreType.REGULAR,
        ],
        compiler_params=pltpu.CompilerParams(
            collective_id=0, has_side_effects=True, vmem_limit_bytes=40 << 20
        ),
        name="block_attention",
    )(queries, rebuilt, out_weight.T, residual, branch_gate.reshape(1, COLS))


def solution(mesh):
    in_specs = (
        P("patch", "heads"),
        P(None, None, "heads"),
        P("patch", None, "heads"),
        P("patch", "heads"),
        P("patch", "heads"),
        P("heads"),
        P("heads", "patch"),
    )
    return jax.shard_map(
        body, mesh=mesh, in_specs=in_specs, out_specs=P("patch", "heads"), check_vma=False
    )
```

```python
import functools
import math

import jax
import jax.numpy as jnp
from jax import lax
from jax.experimental import pallas as pl
from jax.experimental.pallas import tpu as pltpu
from jax.sharding import PartitionSpec as P

MESH = pl.DeviceIdType.MESH
BF16, F32 = jnp.bfloat16, jnp.float32
ROWS, FEAT, HD, NH = 48, 384, 128, 3
COLS, SHARD = 640, 80
KEYS = 1536
NT = (((1,), (1,)), ((), ()))


def place(x, y, z, zh, c):
    return ((x * 8 + z) * 2 + c, zh * 4 + y)


def kernel(
    q_hbm, stale_hbm, codes_hbm, scales_hbm, res_hbm, gate_hbm, w_hbm, out_ref,
    q_ref, stale, codes, scales, res_ref, gate_ref, wt_ref, kvs, kv, qb, osend, orecv, arecv, wcol, wt_far, we, acc, psend, precv,
    k_send, k_recv, kd_send, kd_recv, q_send, q_recv, w_send, w_recv, x_send, x_recv, wd_send, wd_recv,
    o_send, o_recv, a_send, a_recv, p_send, p_recv, in_sem, far_sem,
):
    p, h = lax.axis_index("patch"), lax.axis_index("heads")
    c = lax.rem(p, 2)
    z = lax.rem(lax.div(p, 2), 8)
    x = lax.div(p, 16)
    y = lax.rem(h, 4)
    zh = lax.div(h, 4)
    z0 = lax.rem(z, 4)
    z1 = lax.div(z, 4)
    half = z1 * 4
    other = 4 - half
    across = lax.rem(z + 4, 8)
    worker = x < NH

    x_mates = [lax.rem(x + d, 4) for d in (1, 3, 2)]
    y_mates = [lax.rem(y + d, 4) for d in (1, 3, 2)]
    z_mates = [z0 + 1 - 2 * lax.rem(z0, 2), 3 - z0, lax.rem(z0 + 2, 4)]
    core_dev = place(x, y, z, zh, 1 - c)
    y_devs = [place(x, m, z, zh, c) for m in y_mates]
    z_devs = [place(x, y, half + m, zh, c) for m in z_mates]
    g4 = place(x, y, across, zh, c)
    g8 = place(x, y, z, 1 - zh, c)
    g12 = place(x, y, across, 1 - zh, c)

    sender = lax.div(x, 2) == zh
    w_to = [place(y, lax.rem(x, 2) * 2 + side, z, zh, c) for side in (z1, 1 - z1)]
    w_from = place(zh * 2 + lax.div(y, 2), x, z, zh, c)
    w_self = [sender & (x == y) & (y == lax.rem(x, 2) * 2 + side) for side in (z1, 1 - z1)]
    w_own = w_self[0] | w_self[1]

    loads = [
        pltpu.make_async_copy(src, dst, in_sem.at[i])
        for i, (src, dst) in enumerate(
            (
                (stale_hbm.at[pl.ds(p * ROWS, ROWS)], stale), (codes_hbm, codes), (scales_hbm, scales),
                (w_hbm, wt_ref), (q_hbm, q_ref), (res_hbm, res_ref), (gate_hbm, gate_ref),
            )
        )
    ]
    for load in loads:
        load.start()

    barrier = pltpu.get_barrier_semaphore()

    def greet(target):
        pl.semaphore_signal(barrier, inc=1, device_id=target, device_id_type=MESH)

    for target in [g12, g4, *[place(m, y, across, zh, c) for m in x_mates], *y_devs, core_dev]:
        greet(target)
    for m in (x, *x_mates):
        for target in z_mates:
            greet(place(m, y, half + target, zh, c))
    for m in x_mates:
        greet(place(m, y, z, zh, c))

    @pl.when(jnp.logical_not(w_own))
    def _():
        greet(w_from)

    for i in range(2):
        @pl.when(sender & jnp.logical_not(w_self[i]))
        def _():
            greet(w_to[i])

    for load in loads:
        load.wait()
    lanes = lax.broadcasted_iota(jnp.int32, (ROWS, ROWS), 1)
    diagonal = lax.broadcasted_iota(jnp.int32, (ROWS, ROWS), 0) == lanes
    lines = scales[...].astype(F32)
    factor = [
        jnp.sum(jnp.where(diagonal, lines[e : e + 1], 0.0), axis=1, keepdims=True) for e in range(NH)
    ]
    for side in range(2):
        old, change = stale[:, side].astype(F32), codes[:, side].astype(F32)
        for e in range(NH):
            at = slice(e * HD, (e + 1) * HD)
            kvs[e, :, side * HD : (side + 1) * HD] = (old[:, at] + factor[e] * change[:, at]).astype(BF16)
    own_count = w_own.astype(jnp.int32)
    pl.semaphore_wait(barrier, 25 - 2 * own_count + 2 * sender.astype(jnp.int32))
    pl.semaphore_signal(far_sem, inc=1, device_id=g4, device_id_type=MESH)

    def remote(src, dst, send, recv, target):
        return pltpu.make_async_remote_copy(
            src_ref=src, dst_ref=dst, send_sem=send, recv_sem=recv,
            device_id=target, device_id_type=MESH,
        )

    sent, sent_if = [], []

    def start(copy):
        copy.start()
        sent.append(copy)

    def start_if(condition, copy):
        @pl.when(condition)
        def _():
            copy.start()

        sent_if.append((condition, copy))

    def arrived(block, sem):
        pltpu.make_async_copy(block, block, sem).wait()

    def head_of(e):
        return slice(e * HD, (e + 1) * HD)

    start_if(jnp.logical_not(sender), remote(wt_ref, wt_far, w_send.at[0], w_recv.at[8], g12))
    mine = wcol.at[z]
    w_src = [wt_ref, wt_far]

    def send_shard(i):
        start_if(
            sender & jnp.logical_not(w_self[i]),
            remote(w_src[i], mine, w_send.at[1 + i], w_recv.at[9], w_to[i]),
        )

        @pl.when(w_self[i])
        def _():
            pltpu.make_async_copy(w_src[i], mine, w_recv.at[9]).start()

    send_shard(0)

    for k, m in enumerate((*z_mates[::-1], z0)):
        for e in range(NH):
            copy = remote(
                kvs.at[e], kv.at[c, z0, x], k_send.at[k, e], k_recv.at[z0, x], place(e, y, half + m, zh, c)
            )
            if k < 3:
                start(copy)
            else:
                start_if(x != e, copy)

                @pl.when(x == e)
                def _():
                    pltpu.make_async_copy(kvs.at[e], kv.at[c, z0, x], k_recv.at[z0, x]).start()

    for row, to_z in enumerate((across, z)):
        row = 1 - row
        for e in range(NH):
            copy = remote(
                q_ref.at[:, head_of(e)], qb.at[row, x], q_send.at[row, e], q_recv.at[row, x],
                place(e, y, to_z, zh, c),
            )
            if row == 1:
                start(copy)
            else:
                start_if(x != e, copy)

                @pl.when(x == e)
                def _():
                    pltpu.make_async_copy(q_ref.at[:, head_of(e)], qb.at[0, x], q_recv.at[0, x]).start()

    @pl.when(sender)
    def _():
        arrived(wt_far, w_recv.at[8])

    send_shard(1)

    order = (z0, *z_mates)
    for k, zs in enumerate(order):
        @pl.when(worker)
        def _():
            for m in (x, *x_mates):
                arrived(kv.at[c, zs, m], k_recv.at[zs, m])

        block = kv.at[c, zs]
        start_if(worker, remote(block, block, kd_send.at[k], kd_recv.at[zs], core_dev))
        if k == 1:
            arrived(mine, w_recv.at[9])
            for i, target in enumerate(z_devs):
                start(remote(mine, mine, w_send.at[3 + i], w_recv.at[z], target))
            start(remote(mine, mine, w_send.at[6], w_recv.at[z], g4))

    @pl.when(worker)
    def _():
        for row in range(2):
            for m in (x, *x_mates):
                arrived(qb.at[row, m], q_recv.at[row, m])
        for zs in order:
            arrived(kv.at[1 - c, zs], kd_recv.at[zs])
        keys = kv[:, :, :, :, :HD].reshape(KEYS, HD)
        values = kv[:, :, :, :, HD:].reshape(KEYS, HD)
        wide = lax.broadcasted_iota(jnp.int32, (4 * ROWS, 2 * HD), 1)
        deep = lax.broadcasted_iota(jnp.int32, (4 * ROWS, 2 * HD), 0)
        at_row = lax.broadcasted_iota(jnp.int32, (16, HD), 0)
        for row in range(2):
            levels = []
            for pair in range(2):
                query = qb[row, 2 * pair : 2 * pair + 2].reshape(2 * ROWS, HD)
                scores = lax.dot_general(query, keys, NT, preferred_element_type=F32)
                scores = scores * (1.0 / math.sqrt(HD))
                top = jnp.max(scores, axis=1, keepdims=True)
                exponent = jnp.exp(scores - top)
                total = jnp.sum(exponent, axis=1, keepdims=True)
                mixed = jnp.dot(exponent.astype(BF16), values, preferred_element_type=F32) / total
                osend[row, 2 * pair * ROWS : 2 * (pair + 1) * ROWS] = mixed.astype(BF16)
                levels.append(top + jnp.log(total))
            level = jnp.concatenate(levels, axis=0)
            stats = jnp.zeros((16, HD), F32)
            for t in range(3):
                term = level.astype(BF16).astype(F32)
                level = level - term
                line = jnp.sum(jnp.where(wide == deep, term, 0.0), axis=0, keepdims=True)
                stats = jnp.where(at_row == 2 * t, line[:, :HD], stats)
                stats = jnp.where(at_row == 2 * t + 1, line[:, HD:], stats)
            osend[row, 4 * ROWS :] = stats.astype(BF16)

    pl.semaphore_wait(far_sem, 1)
    for i, (row, target) in enumerate(((0, g8), (1, g12), (1, g4))):
        start_if(worker, remote(osend.at[row], orecv.at[i], o_send.at[i], o_recv.at[i], target))

    def scatter(base, g):
        for e in range(NH):
            block = wcol.at[pl.ds(base, 4), :, head_of(e)]
            dst = we.at[c, x, pl.ds(base, 4)]
            start_if(x != e, remote(block, dst, x_send.at[g, e], x_recv.at[g, x], place(e, y, z, zh, c)))

            @pl.when(x == e)
            def _():
                pltpu.make_async_copy(block, dst, x_recv.at[g, x]).start()

    for m in z_mates:
        arrived(wcol.at[half + m], w_recv.at[half + m])
    scatter(half, 0)
    arrived(wcol.at[across], w_recv.at[across])
    for i, target in enumerate(z_devs):
        block = wcol.at[across]
        start(remote(block, block, w_send.at[7 + i], w_recv.at[across], target))

    def to_core(base, g):
        @pl.when(worker)
        def _():
            for m in (x, *x_mates):
                arrived(we.at[c, m, pl.ds(base, 4)], x_recv.at[g, m])

        block = we.at[c, :, pl.ds(base, 4)]
        start_if(worker, remote(block, block, wd_send.at[g], wd_recv.at[g], core_dev))

    to_core(half, 0)
    for m in z_mates:
        arrived(wcol.at[other + m], w_recv.at[other + m])
    scatter(other, 1)

    def merge(one, two):
        wide = lax.broadcasted_iota(jnp.int32, (4 * ROWS, 2 * HD), 1)
        deep = lax.broadcasted_iota(jnp.int32, (4 * ROWS, 2 * HD), 0)
        levels = []
        for part_of in (one, two):
            stats = part_of[4 * ROWS :].astype(F32)
            line = jnp.concatenate([stats[i : i + 1] + stats[i + 2 : i + 3] + stats[i + 4 : i + 5] for i in range(2)], axis=1)
            levels.append(jnp.sum(jnp.where(wide == deep, line, 0.0), axis=1, keepdims=True))
        high = jnp.maximum(levels[0], levels[1])
        w1, w2 = jnp.exp(levels[0] - high), jnp.exp(levels[1] - high)
        blend = one[: 4 * ROWS].astype(F32) * w1 + two[: 4 * ROWS].astype(F32) * w2
        return (blend / (w1 + w2)).astype(BF16)

    def share(heads_of, k):
        for i, target in enumerate(y_devs):
            block = arecv.at[y, heads_of]
            start_if(worker, remote(block, block, a_send.at[k, i], a_recv.at[y, k], target))

    @pl.when(worker)
    def _():
        arrived(orecv.at[2], o_recv.at[2])
        arecv[y, zh] = merge(osend[0], orecv[2])

    share(zh, 0)

    @pl.when(worker)
    def _():
        arrived(orecv.at[0], o_recv.at[0])
        arrived(orecv.at[1], o_recv.at[1])
        arecv[y, 1 - zh] = merge(orecv[0], orecv[1])

    share(1 - zh, 1)
    to_core(other, 1)

    @pl.when(worker)
    def _():
        arrived(we.at[1 - c, :, pl.ds(half, 4)], wd_recv.at[0])
        arrived(we.at[1 - c, :, pl.ds(other, 4)], wd_recv.at[1])
        for m in y_mates:
            arrived(arecv.at[m, zh], a_recv.at[m, 0])
            arrived(arecv.at[m, 1 - zh], a_recv.at[m, 1])
        rows, weights = [], []
        for m in range(4):
            for side in range(2):
                same = 1 - lax.rem(y + side, 2)
                rows.append(arecv[m, same * zh + (1 - same) * (1 - zh)])
                weights.append(jnp.concatenate([we[j % 2, m, side * 4 + j // 2] for j in range(8)], axis=0))
        total = lax.dot_general(
            jnp.concatenate(rows, axis=1), jnp.concatenate(weights, axis=1), NT, preferred_element_type=F32
        )
        psend[...] = total.astype(BF16).reshape(4, ROWS, COLS)
        for e in range(NH):
            @pl.when(x == e)
            def _():
                acc[...] = total[e * ROWS : (e + 1) * ROWS]

    @pl.when(jnp.logical_not(worker))
    def _():
        acc[...] = jnp.zeros((ROWS, COLS), F32)

    for i, m in enumerate(x_mates):
        start_if(worker, remote(psend.at[m], precv.at[x], p_send.at[i], p_recv.at[x], place(m, y, z, zh, c)))
    for e in range(NH):
        @pl.when(x != e)
        def _():
            arrived(precv.at[e], p_recv.at[e])
            acc[...] += precv[e].astype(F32)

    out_ref[...] = (res_ref[...].astype(F32) + gate_ref[...].reshape(1, COLS) * acc[...]).astype(BF16)

    for copy in sent:
        copy.wait_send()
    for condition, copy in sent_if:
        @pl.when(condition)
        def _():
            copy.wait_send()


def body(queries, stale_pairs, diff_codes, block_scales, residual, branch_gate, out_weight):
    dma = pltpu.SemaphoreType.DMA
    return pl.pallas_call(
        kernel,
        out_shape=jax.ShapeDtypeStruct((ROWS, COLS), BF16),
        in_specs=[pl.BlockSpec(memory_space=pltpu.HBM)] * 7,
        out_specs=pl.BlockSpec(memory_space=pltpu.VMEM),
        scratch_shapes=[
            pltpu.VMEM((ROWS, FEAT), BF16),
            pltpu.VMEM((ROWS, 2, FEAT), BF16),
            pltpu.VMEM((ROWS, 2, FEAT), BF16),
            pltpu.VMEM((NH, ROWS), BF16),
            pltpu.VMEM((ROWS, COLS), BF16),
            pltpu.VMEM((COLS,), F32),
            pltpu.VMEM((SHARD, FEAT), BF16),
            pltpu.VMEM((NH, ROWS, 2 * HD), BF16),
            pltpu.VMEM((2, 4, 4, ROWS, 2 * HD), BF16),
            pltpu.VMEM((2, 4, ROWS, HD), BF16),
            pltpu.VMEM((2, 4 * ROWS + 16, HD), BF16),
            pltpu.VMEM((3, 4 * ROWS + 16, HD), BF16),
            pltpu.VMEM((4, 2, 4 * ROWS, HD), BF16),
            pltpu.VMEM((8, SHARD, FEAT), BF16),
            pltpu.VMEM((SHARD, FEAT), BF16),
            pltpu.VMEM((2, 4, 8, SHARD, HD), BF16),
            pltpu.VMEM((ROWS, COLS), F32),
            pltpu.VMEM((4, ROWS, COLS), BF16),
            pltpu.VMEM((NH, ROWS, COLS), BF16),
            dma((4, NH)), dma((4, 4)), dma((4,)), dma((4,)), dma((2, NH)), dma((2, 4)), dma((10,)), dma((10,)),
            dma((2, NH)), dma((2, 4)), dma((2,)), dma((2,)),
            dma((3,)), dma((3,)), dma((2, 3)), dma((4, 2)), dma((3,)), dma((3,)), dma((7,)), pltpu.SemaphoreType.REGULAR,
        ],
        compiler_params=pltpu.CompilerParams(
            collective_id=0, has_side_effects=True, vmem_limit_bytes=60 << 20
        ),
        name="block_attention",
    )(queries, stale_pairs, diff_codes, block_scales.T, residual, branch_gate, out_weight.T)


def solution(mesh):
    in_specs = (
        P("patch", "heads"),
        P(None, None, "heads"),
        P("patch", None, "heads"),
        P("patch", "heads"),
        P("patch", "heads"),
        P("heads"),
        P("heads", "patch"),
    )
    return jax.shard_map(
        body, mesh=mesh, in_specs=in_specs, out_specs=P("patch", "heads"), check_vma=False
    )
```

```python
import functools
import math

import jax
import jax.numpy as jnp
from jax import lax
from jax.experimental import pallas as pl
from jax.experimental.pallas import tpu as pltpu
from jax.sharding import PartitionSpec as P

MESH = pl.DeviceIdType.MESH
BF16, F32 = jnp.bfloat16, jnp.float32
ROWS, FEAT, HD, NH = 48, 384, 128, 3
COLS, SHARD = 640, 80
KEYS = 1536
NT = (((1,), (1,)), ((), ()))


def place(x, y, z, zh, c):
    return ((x * 8 + z) * 2 + c, zh * 4 + y)


def kernel(
    q_hbm, stale_hbm, codes_hbm, scales_hbm, res_hbm, gate_hbm, w_hbm, out_ref,
    q_ref, stale, codes, scales, res_ref, gate_ref, wt_ref, kvs, kv, qb, osend, orecv, att, arecv, wcol, wt_far, we, part, psend, precv,
    k_send, k_recv, kd_send, kd_recv, q_send, q_recv, w_send, w_recv, x_send, x_recv, wd_send, wd_recv,
    o_send, o_recv, a_send, a_recv, p_send, p_recv, in_sem, far_sem,
):
    p, h = lax.axis_index("patch"), lax.axis_index("heads")
    c = lax.rem(p, 2)
    z = lax.rem(lax.div(p, 2), 8)
    x = lax.div(p, 16)
    y = lax.rem(h, 4)
    zh = lax.div(h, 4)
    z0 = lax.rem(z, 4)
    z1 = lax.div(z, 4)
    half = z1 * 4
    other = 4 - half
    across = lax.rem(z + 4, 8)
    worker = x < NH

    x_mates = [lax.rem(x + d, 4) for d in (1, 3, 2)]
    y_mates = [lax.rem(y + d, 4) for d in (1, 3, 2)]
    z_mates = [z0 + 1 - 2 * lax.rem(z0, 2), 3 - z0, lax.rem(z0 + 2, 4)]
    core_dev = place(x, y, z, zh, 1 - c)
    y_devs = [place(x, m, z, zh, c) for m in y_mates]
    z_devs = [place(x, y, half + m, zh, c) for m in z_mates]
    g4 = place(x, y, across, zh, c)
    g8 = place(x, y, z, 1 - zh, c)
    g12 = place(x, y, across, 1 - zh, c)

    sender = lax.div(x, 2) == zh
    w_to = [place(y, lax.rem(x, 2) * 2 + side, z, zh, c) for side in (z1, 1 - z1)]
    w_from = place(zh * 2 + lax.div(y, 2), x, z, zh, c)
    w_self = [sender & (x == y) & (y == lax.rem(x, 2) * 2 + side) for side in (z1, 1 - z1)]
    w_own = w_self[0] | w_self[1]

    loads = [
        pltpu.make_async_copy(src, dst, in_sem.at[i])
        for i, (src, dst) in enumerate(
            (
                (stale_hbm.at[pl.ds(p * ROWS, ROWS)], stale), (codes_hbm, codes), (scales_hbm, scales),
                (w_hbm, wt_ref), (q_hbm, q_ref), (res_hbm, res_ref), (gate_hbm, gate_ref),
            )
        )
    ]
    for load in loads:
        load.start()

    barrier = pltpu.get_barrier_semaphore()

    def greet(target):
        pl.semaphore_signal(barrier, inc=1, device_id=target, device_id_type=MESH)

    for target in [g12, g4, *[place(m, y, across, zh, c) for m in x_mates], *y_devs, core_dev]:
        greet(target)
    for m in (x, *x_mates):
        for target in z_mates:
            greet(place(m, y, half + target, zh, c))
    for m in x_mates:
        greet(place(m, y, z, zh, c))

    @pl.when(jnp.logical_not(w_own))
    def _():
        greet(w_from)

    for i in range(2):
        @pl.when(sender & jnp.logical_not(w_self[i]))
        def _():
            greet(w_to[i])

    for load in loads:
        load.wait()
    lanes = lax.broadcasted_iota(jnp.int32, (ROWS, ROWS), 1)
    diagonal = lax.broadcasted_iota(jnp.int32, (ROWS, ROWS), 0) == lanes
    lines = scales[...].astype(F32)
    factor = [
        jnp.sum(jnp.where(diagonal, lines[e : e + 1], 0.0), axis=1, keepdims=True) for e in range(NH)
    ]
    for side in range(2):
        old, change = stale[:, side].astype(F32), codes[:, side].astype(F32)
        for e in range(NH):
            at = slice(e * HD, (e + 1) * HD)
            kvs[e, :, side * HD : (side + 1) * HD] = (old[:, at] + factor[e] * change[:, at]).astype(BF16)
    own_count = w_own.astype(jnp.int32)
    pl.semaphore_wait(barrier, 25 - 2 * own_count + 2 * sender.astype(jnp.int32))
    pl.semaphore_signal(far_sem, inc=1, device_id=g4, device_id_type=MESH)

    def remote(src, dst, send, recv, target):
        return pltpu.make_async_remote_copy(
            src_ref=src, dst_ref=dst, send_sem=send, recv_sem=recv,
            device_id=target, device_id_type=MESH,
        )

    sent, sent_if = [], []

    def start(copy):
        copy.start()
        sent.append(copy)

    def start_if(condition, copy):
        @pl.when(condition)
        def _():
            copy.start()

        sent_if.append((condition, copy))

    def arrived(block, sem):
        pltpu.make_async_copy(block, block, sem).wait()

    def head_of(e):
        return slice(e * HD, (e + 1) * HD)

    start_if(jnp.logical_not(sender), remote(wt_ref, wt_far, w_send.at[0], w_recv.at[8], g12))
    mine = wcol.at[z]
    w_src = [wt_ref, wt_far]

    def send_shard(i):
        start_if(
            sender & jnp.logical_not(w_self[i]),
            remote(w_src[i], mine, w_send.at[1 + i], w_recv.at[9], w_to[i]),
        )

        @pl.when(w_self[i])
        def _():
            pltpu.make_async_copy(w_src[i], mine, w_recv.at[9]).start()

    send_shard(0)

    for k, m in enumerate((*z_mates[::-1], z0)):
        for e in range(NH):
            copy = remote(
                kvs.at[e], kv.at[c, z0, x], k_send.at[k, e], k_recv.at[z0, x], place(e, y, half + m, zh, c)
            )
            if k < 3:
                start(copy)
            else:
                start_if(x != e, copy)

                @pl.when(x == e)
                def _():
                    pltpu.make_async_copy(kvs.at[e], kv.at[c, z0, x], k_recv.at[z0, x]).start()

    for row, to_z in enumerate((across, z)):
        row = 1 - row
        for e in range(NH):
            copy = remote(
                q_ref.at[:, head_of(e)], qb.at[row, x], q_send.at[row, e], q_recv.at[row, x],
                place(e, y, to_z, zh, c),
            )
            if row == 1:
                start(copy)
            else:
                start_if(x != e, copy)

                @pl.when(x == e)
                def _():
                    pltpu.make_async_copy(q_ref.at[:, head_of(e)], qb.at[0, x], q_recv.at[0, x]).start()

    order = (z0, *z_mates)

    def spread(at, g):
        for k, m in enumerate((*z_mates[::-1], z0)):
            for e in range(NH):
                column = jnp.where(x == y, 3, e)
                slot = jnp.where(x == y, e, lax.rem(x - y + 3, 4))
                block, dst, sem = wcol.at[at, :, head_of(e)], we.at[c, slot, at], x_recv.at[slot, at]
                copy = remote(block, dst, x_send.at[g, k, e], sem, place(column, y, half + m, zh, c))
                if k < 3:
                    start(copy)
                else:
                    start_if(x != column, copy)

                    @pl.when(x == column)
                    def _():
                        pltpu.make_async_copy(block, dst, sem).start()

    for k, zs in enumerate(order):
        @pl.when(worker)
        def _():
            for m in (x, *x_mates):
                arrived(kv.at[c, zs, m], k_recv.at[zs, m])

        block = kv.at[c, zs]
        start_if(worker, remote(block, block, kd_send.at[k], kd_recv.at[zs], core_dev))
        if k == 0:
            @pl.when(sender)
            def _():
                arrived(wt_far, w_recv.at[8])

            send_shard(1)

        if k == 1:
            arrived(mine, w_recv.at[9])
            start(remote(mine, mine, w_send.at[3], w_recv.at[z], g4))

    spread(z, 0)

    @pl.when(worker)
    def _():
        for row in range(2):
            for m in (x, *x_mates):
                arrived(qb.at[row, m], q_recv.at[row, m])
        for zs in order:
            arrived(kv.at[1 - c, zs], kd_recv.at[zs])
        keys = kv[:, :, :, :, :HD].reshape(KEYS, HD)
        values = kv[:, :, :, :, HD:].reshape(KEYS, HD)
        wide = lax.broadcasted_iota(jnp.int32, (4 * ROWS, 2 * HD), 1)
        deep = lax.broadcasted_iota(jnp.int32, (4 * ROWS, 2 * HD), 0)
        at_row = lax.broadcasted_iota(jnp.int32, (16, HD), 0)
        for row in range(2):
            levels = []
            for pair in range(2):
                query = qb[row, 2 * pair : 2 * pair + 2].reshape(2 * ROWS, HD)
                scores = lax.dot_general(query, keys, NT, preferred_element_type=F32)
                scores = scores * (1.0 / math.sqrt(HD))
                top = jnp.max(scores, axis=1, keepdims=True)
                exponent = jnp.exp(scores - top)
                total = jnp.sum(exponent, axis=1, keepdims=True)
                mixed = jnp.dot(exponent.astype(BF16), values, preferred_element_type=F32) / total
                osend[row, 2 * pair * ROWS : 2 * (pair + 1) * ROWS] = mixed.astype(BF16)
                levels.append(top + jnp.log(total))
            level = jnp.concatenate(levels, axis=0)
            stats = jnp.zeros((16, HD), F32)
            for t in range(3):
                term = level.astype(BF16).astype(F32)
                level = level - term
                line = jnp.sum(jnp.where(wide == deep, term, 0.0), axis=0, keepdims=True)
                stats = jnp.where(at_row == 2 * t, line[:, :HD], stats)
                stats = jnp.where(at_row == 2 * t + 1, line[:, HD:], stats)
            osend[row, 4 * ROWS :] = stats.astype(BF16)

    pl.semaphore_wait(far_sem, 1)
    for i, (row, target) in enumerate(((0, g8), (1, g12), (1, g4))):
        start_if(worker, remote(osend.at[row], orecv.at[i], o_send.at[i], o_recv.at[i], target))

    arrived(wcol.at[across], w_recv.at[across])
    spread(across, 1)

    def to_core(base, g):
        for slot in range(3):
            for zs in order:
                arrived(we.at[c, slot, base + zs], x_recv.at[slot, base + zs])
        block = we.at[c, :, pl.ds(base, 4)]
        start(remote(block, block, wd_send.at[g], wd_recv.at[g], core_dev))

    to_core(half, 0)

    def merge(one, two):
        wide = lax.broadcasted_iota(jnp.int32, (4 * ROWS, 2 * HD), 1)
        deep = lax.broadcasted_iota(jnp.int32, (4 * ROWS, 2 * HD), 0)
        levels = []
        for part_of in (one, two):
            stats = part_of[4 * ROWS :].astype(F32)
            line = jnp.concatenate([stats[i : i + 1] + stats[i + 2 : i + 3] + stats[i + 4 : i + 5] for i in range(2)], axis=1)
            levels.append(jnp.sum(jnp.where(wide == deep, line, 0.0), axis=1, keepdims=True))
        high = jnp.maximum(levels[0], levels[1])
        w1, w2 = jnp.exp(levels[0] - high), jnp.exp(levels[1] - high)
        blend = one[: 4 * ROWS].astype(F32) * w1 + two[: 4 * ROWS].astype(F32) * w2
        return (blend / (w1 + w2)).astype(BF16)

    def share(heads_of, k):
        block = att.at[heads_of]
        for d in (1, 3, 2):
            target = place(x, lax.rem(y + d, 4), z, zh, c)
            dst = arecv.at[3 - d, heads_of]
            start_if(worker, remote(block, dst, a_send.at[k, d - 1], a_recv.at[3 - d, k], target))
        slot = lax.rem(x, 3)
        dst = arecv.at[slot, heads_of]
        start_if(worker, remote(block, dst, a_send.at[k, 3], a_recv.at[slot, k], place(3, y, z, zh, c)))

    @pl.when(worker)
    def _():
        arrived(orecv.at[2], o_recv.at[2])
        att[zh] = merge(osend[0], orecv[2])

    share(zh, 0)

    @pl.when(worker)
    def _():
        arrived(orecv.at[0], o_recv.at[0])
        arrived(orecv.at[1], o_recv.at[1])
        att[1 - zh] = merge(orecv[0], orecv[1])

    share(1 - zh, 1)
    to_core(other, 1)

    arrived(we.at[1 - c, :, pl.ds(half, 4)], wd_recv.at[0])
    arrived(we.at[1 - c, :, pl.ds(other, 4)], wd_recv.at[1])
    rows, weights = [], []
    for m in range(3):
        arrived(arecv.at[m, zh], a_recv.at[m, 0])
        arrived(arecv.at[m, 1 - zh], a_recv.at[m, 1])
    for m in range(3):
        for side in range(2):
            same = 1 - lax.rem(y + side, 2)
            rows.append(arecv[m, same * zh + (1 - same) * (1 - zh)])
            weights.append(jnp.concatenate([we[j % 2, m, side * 4 + j // 2] for j in range(8)], axis=0))
    total = lax.dot_general(
        jnp.concatenate(rows, axis=1), jnp.concatenate(weights, axis=1), NT, preferred_element_type=F32
    )
    part[...] = total.reshape(4, ROWS, COLS)
    psend[...] = total.astype(BF16).reshape(4, ROWS, COLS)
    for i, m in enumerate(x_mates):
        start(remote(psend.at[m], precv.at[x], p_send.at[i], p_recv.at[x], place(m, y, z, zh, c)))
    summed = part[x]
    for m in x_mates:
        arrived(precv.at[m], p_recv.at[m])
        summed = summed + precv[m].astype(F32)
    out_ref[...] = (res_ref[...].astype(F32) + gate_ref[...].reshape(1, COLS) * summed).astype(BF16)

    for copy in sent:
        copy.wait_send()
    for condition, copy in sent_if:
        @pl.when(condition)
        def _():
            copy.wait_send()


def body(queries, stale_pairs, diff_codes, block_scales, residual, branch_gate, out_weight):
    dma = pltpu.SemaphoreType.DMA
    return pl.pallas_call(
        kernel,
        out_shape=jax.ShapeDtypeStruct((ROWS, COLS), BF16),
        in_specs=[pl.BlockSpec(memory_space=pltpu.HBM)] * 7,
        out_specs=pl.BlockSpec(memory_space=pltpu.VMEM),
        scratch_shapes=[
            pltpu.VMEM((ROWS, FEAT), BF16),
            pltpu.VMEM((ROWS, 2, FEAT), BF16),
            pltpu.VMEM((ROWS, 2, FEAT), BF16),
            pltpu.VMEM((NH, ROWS), BF16),
            pltpu.VMEM((ROWS, COLS), BF16),
            pltpu.VMEM((COLS,), F32),
            pltpu.VMEM((SHARD, FEAT), BF16),
            pltpu.VMEM((NH, ROWS, 2 * HD), BF16),
            pltpu.VMEM((2, 4, 4, ROWS, 2 * HD), BF16),
            pltpu.VMEM((2, 4, ROWS, HD), BF16),
            pltpu.VMEM((2, 4 * ROWS + 16, HD), BF16),
            pltpu.VMEM((3, 4 * ROWS + 16, HD), BF16),
            pltpu.VMEM((2, 4 * ROWS, HD), BF16),
            pltpu.VMEM((3, 2, 4 * ROWS, HD), BF16),
            pltpu.VMEM((8, SHARD, FEAT), BF16),
            pltpu.VMEM((SHARD, FEAT), BF16),
            pltpu.VMEM((2, 3, 8, SHARD, HD), BF16),
            pltpu.VMEM((4, ROWS, COLS), F32),
            pltpu.VMEM((4, ROWS, COLS), BF16),
            pltpu.VMEM((4, ROWS, COLS), BF16),
            dma((4, NH)), dma((4, 4)), dma((4,)), dma((4,)), dma((2, NH)), dma((2, 4)), dma((4,)), dma((10,)),
            dma((2, 4, NH)), dma((3, 8)), dma((2,)), dma((2,)),
            dma((3,)), dma((3,)), dma((2, 4)), dma((3, 2)), dma((3,)), dma((4,)), dma((7,)), pltpu.SemaphoreType.REGULAR,
        ],
        compiler_params=pltpu.CompilerParams(
            collective_id=0, has_side_effects=True, vmem_limit_bytes=60 << 20
        ),
        name="block_attention",
    )(queries, stale_pairs, diff_codes, block_scales.T, residual, branch_gate, out_weight.T)


def solution(mesh):
    in_specs = (
        P("patch", "heads"),
        P(None, None, "heads"),
        P("patch", None, "heads"),
        P("patch", "heads"),
        P("patch", "heads"),
        P("heads"),
        P("heads", "patch"),
    )
    return jax.shard_map(
        body, mesh=mesh, in_specs=in_specs, out_specs=P("patch", "heads"), check_vma=False
    )
```

```python
import functools
import math

import jax
import jax.numpy as jnp
from jax import lax
from jax.experimental import pallas as pl
from jax.experimental.pallas import tpu as pltpu
from jax.sharding import PartitionSpec as P

MESH = pl.DeviceIdType.MESH
BF16, F32 = jnp.bfloat16, jnp.float32
ROWS, FEAT, HD, NH = 48, 384, 128, 3
COLS, SHARD = 640, 80
KEYS = 1536
NT = (((1,), (1,)), ((), ()))


def place(x, y, z, zh, c):
    return ((x * 8 + z) * 2 + c, zh * 4 + y)


def kernel(
    q_hbm, stale_hbm, codes_hbm, scales_hbm, w_hbm, out_ref,
    q_ref, stale, codes, scales, wt_ref, kvs, kv, qb, osend, orecv, att, arecv, wcol, wt_far, we, part, psend, precv,
    k_send, k_recv, kd_send, kd_recv, q_send, q_recv, w_send, w_recv, x_send, x_recv, wd_send, wd_recv,
    o_send, o_recv, a_send, a_recv, p_send, p_recv, in_sem, far_sem,
):
    p, h = lax.axis_index("patch"), lax.axis_index("heads")
    c = lax.rem(p, 2)
    z = lax.rem(lax.div(p, 2), 8)
    x = lax.div(p, 16)
    y = lax.rem(h, 4)
    zh = lax.div(h, 4)
    z0 = lax.rem(z, 4)
    z1 = lax.div(z, 4)
    half = z1 * 4
    other = 4 - half
    across = lax.rem(z + 4, 8)
    worker = x < NH

    x_mates = [lax.rem(x + d, 4) for d in (1, 3, 2)]
    y_mates = [lax.rem(y + d, 4) for d in (1, 3, 2)]
    z_mates = [z0 + 1 - 2 * lax.rem(z0, 2), 3 - z0, lax.rem(z0 + 2, 4)]
    core_dev = place(x, y, z, zh, 1 - c)
    y_devs = [place(x, m, z, zh, c) for m in y_mates]
    z_devs = [place(x, y, half + m, zh, c) for m in z_mates]
    g4 = place(x, y, across, zh, c)
    g8 = place(x, y, z, 1 - zh, c)
    g12 = place(x, y, across, 1 - zh, c)

    sender = lax.div(x, 2) == zh
    w_to = [place(y, lax.rem(x, 2) * 2 + side, z, zh, c) for side in (z1, 1 - z1)]
    w_from = place(zh * 2 + lax.div(y, 2), x, z, zh, c)
    w_self = [sender & (x == y) & (y == lax.rem(x, 2) * 2 + side) for side in (z1, 1 - z1)]
    w_own = w_self[0] | w_self[1]

    loads = [
        pltpu.make_async_copy(src, dst, in_sem.at[i])
        for i, (src, dst) in enumerate(
            (
                (stale_hbm.at[pl.ds(p * ROWS, ROWS)], stale), (codes_hbm, codes), (scales_hbm, scales),
                (w_hbm, wt_ref), (q_hbm, q_ref),
            )
        )
    ]
    for load in loads:
        load.start()

    barrier = pltpu.get_barrier_semaphore()

    def greet(target):
        pl.semaphore_signal(barrier, inc=1, device_id=target, device_id_type=MESH)

    for target in [g12, g4, *[place(m, y, across, zh, c) for m in x_mates], *y_devs, core_dev]:
        greet(target)
    for m in (x, *x_mates):
        for target in z_mates:
            greet(place(m, y, half + target, zh, c))
    for m in x_mates:
        greet(place(m, y, z, zh, c))

    @pl.when(jnp.logical_not(w_own))
    def _():
        greet(w_from)

    for i in range(2):
        @pl.when(sender & jnp.logical_not(w_self[i]))
        def _():
            greet(w_to[i])

    for load in loads:
        load.wait()
    lanes = lax.broadcasted_iota(jnp.int32, (ROWS, ROWS), 1)
    diagonal = lax.broadcasted_iota(jnp.int32, (ROWS, ROWS), 0) == lanes
    lines = scales[...].astype(F32)
    factor = [
        jnp.sum(jnp.where(diagonal, lines[e : e + 1], 0.0), axis=1, keepdims=True) for e in range(NH)
    ]
    for side in range(2):
        old, change = stale[:, side].astype(F32), codes[:, side].astype(F32)
        for e in range(NH):
            at = slice(e * HD, (e + 1) * HD)
            kvs[e, :, side * HD : (side + 1) * HD] = (old[:, at] + factor[e] * change[:, at]).astype(BF16)
    own_count = w_own.astype(jnp.int32)
    pl.semaphore_wait(barrier, 25 - 2 * own_count + 2 * sender.astype(jnp.int32))
    pl.semaphore_signal(far_sem, inc=1, device_id=g4, device_id_type=MESH)

    def remote(src, dst, send, recv, target):
        return pltpu.make_async_remote_copy(
            src_ref=src, dst_ref=dst, send_sem=send, recv_sem=recv,
            device_id=target, device_id_type=MESH,
        )

    sent, sent_if = [], []

    def start(copy):
        copy.start()
        sent.append(copy)

    def start_if(condition, copy):
        @pl.when(condition)
        def _():
            copy.start()

        sent_if.append((condition, copy))

    def arrived(block, sem):
        pltpu.make_async_copy(block, block, sem).wait()

    def head_of(e):
        return slice(e * HD, (e + 1) * HD)

    start_if(jnp.logical_not(sender), remote(wt_ref, wt_far, w_send.at[0], w_recv.at[8], g12))
    mine = wcol.at[z]
    w_src = [wt_ref, wt_far]

    def send_shard(i):
        start_if(
            sender & jnp.logical_not(w_self[i]),
            remote(w_src[i], mine, w_send.at[1 + i], w_recv.at[9], w_to[i]),
        )

        @pl.when(w_self[i])
        def _():
            pltpu.make_async_copy(w_src[i], mine, w_recv.at[9]).start()

    send_shard(0)

    for k, m in enumerate((*z_mates[::-1], z0)):
        for e in range(NH):
            copy = remote(
                kvs.at[e], kv.at[c, z0, x], k_send.at[k, e], k_recv.at[z0, x], place(e, y, half + m, zh, c)
            )
            if k < 3:
                start(copy)
            else:
                start_if(x != e, copy)

                @pl.when(x == e)
                def _():
                    pltpu.make_async_copy(kvs.at[e], kv.at[c, z0, x], k_recv.at[z0, x]).start()

    for row, to_z in enumerate((across, z)):
        row = 1 - row
        for e in range(NH):
            copy = remote(
                q_ref.at[:, head_of(e)], qb.at[row, x], q_send.at[row, e], q_recv.at[row, x],
                place(e, y, to_z, zh, c),
            )
            if row == 1:
                start(copy)
            else:
                start_if(x != e, copy)

                @pl.when(x == e)
                def _():
                    pltpu.make_async_copy(q_ref.at[:, head_of(e)], qb.at[0, x], q_recv.at[0, x]).start()

    order = (z0, *z_mates)

    def spread(at, g):
        for k, m in enumerate((*z_mates, z0)):
            for e in range(NH):
                column = jnp.where(x == y, 3, e)
                slot = jnp.where(x == y, e, lax.rem(x - y + 3, 4))
                block, dst, sem = wcol.at[at, :, head_of(e)], we.at[c, slot, at], x_recv.at[slot, at]
                copy = remote(block, dst, x_send.at[g, k, e], sem, place(column, y, half + m, zh, c))
                if k < 3:
                    start(copy)
                else:
                    start_if(x != column, copy)

                    @pl.when(x == column)
                    def _():
                        pltpu.make_async_copy(block, dst, sem).start()

    for k, zs in enumerate(order):
        @pl.when(worker)
        def _():
            for m in (x, *x_mates):
                arrived(kv.at[c, zs, m], k_recv.at[zs, m])

        block = kv.at[c, zs]
        start_if(worker, remote(block, block, kd_send.at[k], kd_recv.at[zs], core_dev))
        if k == 0:
            @pl.when(sender)
            def _():
                arrived(wt_far, w_recv.at[8])

            send_shard(1)

        if k == 1:
            arrived(mine, w_recv.at[9])
            start(remote(mine, mine, w_send.at[3], w_recv.at[z], g4))

    spread(z, 0)

    @pl.when(worker)
    def _():
        for row in range(2):
            for m in (x, *x_mates):
                arrived(qb.at[row, m], q_recv.at[row, m])
        for zs in order:
            arrived(kv.at[1 - c, zs], kd_recv.at[zs])

    def attend(row):
        keys = kv[:, :, :, :, :HD].reshape(KEYS, HD)
        values = kv[:, :, :, :, HD:].reshape(KEYS, HD)
        wide = lax.broadcasted_iota(jnp.int32, (4 * ROWS, 2 * HD), 1)
        deep = lax.broadcasted_iota(jnp.int32, (4 * ROWS, 2 * HD), 0)
        at_row = lax.broadcasted_iota(jnp.int32, (16, HD), 0)
        levels = []
        for pair in range(2):
            query = qb[row, 2 * pair : 2 * pair + 2].reshape(2 * ROWS, HD)
            scores = lax.dot_general(query, keys, NT, preferred_element_type=F32)
            scores = scores * (1.0 / math.sqrt(HD))
            top = jnp.max(scores, axis=1, keepdims=True)
            exponent = jnp.exp(scores - top)
            total = jnp.sum(exponent, axis=1, keepdims=True)
            mixed = jnp.dot(exponent.astype(BF16), values, preferred_element_type=F32) / total
            osend[row, 2 * pair * ROWS : 2 * (pair + 1) * ROWS] = mixed.astype(BF16)
            levels.append(top + jnp.log(total))
        level = jnp.concatenate(levels, axis=0)
        stats = jnp.zeros((16, HD), F32)
        for t in range(3):
            term = level.astype(BF16).astype(F32)
            level = level - term
            line = jnp.sum(jnp.where(wide == deep, term, 0.0), axis=0, keepdims=True)
            stats = jnp.where(at_row == 2 * t, line[:, :HD], stats)
            stats = jnp.where(at_row == 2 * t + 1, line[:, HD:], stats)
        osend[row, 4 * ROWS :] = stats.astype(BF16)

    def pass_on(i, row, target):
        start_if(worker, remote(osend.at[row], orecv.at[i], o_send.at[i], o_recv.at[i], target))

    pl.semaphore_wait(far_sem, 1)

    @pl.when(worker)
    def _():
        attend(0)

    pass_on(0, 0, g8)

    @pl.when(worker)
    def _():
        attend(1)

    pass_on(1, 1, g12)
    pass_on(2, 1, g4)

    arrived(wcol.at[across], w_recv.at[across])
    spread(across, 1)

    def to_core(base, g):
        for slot in range(3):
            for zs in order:
                arrived(we.at[c, slot, base + zs], x_recv.at[slot, base + zs])
            block = we.at[c, slot, pl.ds(base, 4)]
            start(remote(block, block, wd_send.at[g, slot], wd_recv.at[g, slot], core_dev))

    to_core(half, 0)

    def merge(one, two):
        wide = lax.broadcasted_iota(jnp.int32, (4 * ROWS, 2 * HD), 1)
        deep = lax.broadcasted_iota(jnp.int32, (4 * ROWS, 2 * HD), 0)
        levels = []
        for part_of in (one, two):
            stats = part_of[4 * ROWS :].astype(F32)
            line = jnp.concatenate([stats[i : i + 1] + stats[i + 2 : i + 3] + stats[i + 4 : i + 5] for i in range(2)], axis=1)
            levels.append(jnp.sum(jnp.where(wide == deep, line, 0.0), axis=1, keepdims=True))
        high = jnp.maximum(levels[0], levels[1])
        w1, w2 = jnp.exp(levels[0] - high), jnp.exp(levels[1] - high)
        blend = one[: 4 * ROWS].astype(F32) * w1 + two[: 4 * ROWS].astype(F32) * w2
        return (blend / (w1 + w2)).astype(BF16)

    def share(heads_of, k):
        block = att.at[heads_of]
        for d in (1, 3, 2):
            target = place(x, lax.rem(y + d, 4), z, zh, c)
            dst = arecv.at[3 - d, heads_of]
            start_if(worker, remote(block, dst, a_send.at[k, d - 1], a_recv.at[3 - d, k], target))
        slot = lax.rem(x, 3)
        dst = arecv.at[slot, heads_of]
        start_if(worker, remote(block, dst, a_send.at[k, 3], a_recv.at[slot, k], place(3, y, z, zh, c)))

    @pl.when(worker)
    def _():
        arrived(orecv.at[2], o_recv.at[2])
        att[zh] = merge(osend[0], orecv[2])

    share(zh, 0)

    @pl.when(worker)
    def _():
        arrived(orecv.at[0], o_recv.at[0])
        arrived(orecv.at[1], o_recv.at[1])
        att[1 - zh] = merge(orecv[0], orecv[1])

    share(1 - zh, 1)
    to_core(other, 1)

    for g, base in enumerate((half, other)):
        for slot in range(3):
            arrived(we.at[1 - c, slot, pl.ds(base, 4)], wd_recv.at[g, slot])
    rows, weights = [], []
    for m in range(3):
        arrived(arecv.at[m, zh], a_recv.at[m, 0])
        arrived(arecv.at[m, 1 - zh], a_recv.at[m, 1])
    for m in range(3):
        for side in range(2):
            same = 1 - lax.rem(y + side, 2)
            rows.append(arecv[m, same * zh + (1 - same) * (1 - zh)])
            weights.append(jnp.concatenate([we[j % 2, m, side * 4 + j // 2] for j in range(8)], axis=0))
    total = lax.dot_general(
        jnp.concatenate(rows, axis=1), jnp.concatenate(weights, axis=1), NT, preferred_element_type=F32
    )
    part[...] = total.reshape(4, ROWS, COLS)
    psend[...] = total.astype(BF16).reshape(4, ROWS, COLS)
    for i, m in enumerate(x_mates):
        start(remote(psend.at[m], precv.at[x], p_send.at[i], p_recv.at[x], place(m, y, z, zh, c)))
    summed = part[x]
    for m in x_mates:
        arrived(precv.at[m], p_recv.at[m])
        summed = summed + precv[m].astype(F32)
    out_ref[...] = summed

    for copy in sent:
        copy.wait_send()
    for condition, copy in sent_if:
        @pl.when(condition)
        def _():
            copy.wait_send()


def body(queries, stale_pairs, diff_codes, block_scales, residual, branch_gate, out_weight):
    dma = pltpu.SemaphoreType.DMA
    summed = pl.pallas_call(
        kernel,
        out_shape=jax.ShapeDtypeStruct((ROWS, COLS), F32),
        in_specs=[pl.BlockSpec(memory_space=pltpu.HBM)] * 5,
        out_specs=pl.BlockSpec(memory_space=pltpu.VMEM),
        scratch_shapes=[
            pltpu.VMEM((ROWS, FEAT), BF16),
            pltpu.VMEM((ROWS, 2, FEAT), BF16),
            pltpu.VMEM((ROWS, 2, FEAT), BF16),
            pltpu.VMEM((NH, ROWS), BF16),
            pltpu.VMEM((SHARD, FEAT), BF16),
            pltpu.VMEM((NH, ROWS, 2 * HD), BF16),
            pltpu.VMEM((2, 4, 4, ROWS, 2 * HD), BF16),
            pltpu.VMEM((2, 4, ROWS, HD), BF16),
            pltpu.VMEM((2, 4 * ROWS + 16, HD), BF16),
            pltpu.VMEM((3, 4 * ROWS + 16, HD), BF16),
            pltpu.VMEM((2, 4 * ROWS, HD), BF16),
            pltpu.VMEM((3, 2, 4 * ROWS, HD), BF16),
            pltpu.VMEM((8, SHARD, FEAT), BF16),
            pltpu.VMEM((SHARD, FEAT), BF16),
            pltpu.VMEM((2, 3, 8, SHARD, HD), BF16),
            pltpu.VMEM((4, ROWS, COLS), F32),
            pltpu.VMEM((4, ROWS, COLS), BF16),
            pltpu.VMEM((4, ROWS, COLS), BF16),
            dma((4, NH)), dma((4, 4)), dma((4,)), dma((4,)), dma((2, NH)), dma((2, 4)), dma((4,)), dma((10,)),
            dma((2, 4, NH)), dma((3, 8)), dma((2, 3)), dma((2, 3)),
            dma((3,)), dma((3,)), dma((2, 4)), dma((3, 2)), dma((3,)), dma((4,)), dma((5,)), pltpu.SemaphoreType.REGULAR,
        ],
        compiler_params=pltpu.CompilerParams(
            collective_id=0, has_side_effects=True, vmem_limit_bytes=60 << 20
        ),
        name="block_attention",
    )(queries, stale_pairs, diff_codes, block_scales.T, out_weight.T)
    return (residual.astype(F32) + branch_gate[None, :] * summed).astype(BF16)


def solution(mesh):
    in_specs = (
        P("patch", "heads"),
        P(None, None, "heads"),
        P("patch", None, "heads"),
        P("patch", "heads"),
        P("patch", "heads"),
        P("heads"),
        P("heads", "patch"),
    )
    return jax.shard_map(
        body, mesh=mesh, in_specs=in_specs, out_specs=P("patch", "heads"), check_vma=False
    )
```
